128 devices in a mesh: row: 16 (over x, z_hi, core), col: 8 (over y, z_lo).
Axes of the slice: x: 4, y: 4, z: 4 (z_hi: 2, z_lo: 2; z = z_hi * 2 + z_lo), core: 2. Of those that a mesh axis runs over, the one named last changes fastest.
Arguments:
- context: bfloat16 [4096, 16384], P('row', 'col'), may hold values from -6 to 6
- out_weight: bfloat16 [16384, 16384], P('col', 'row'), may hold values from -0.046875 to 0.046875
- residual: bfloat16 [4096, 16384], P('col', 'row')
- norm_gain: float32 [16384], P('row'), may hold values from 0.25 to 1.75
- span_lengths: int32 [8, 384], P('col'), may hold values from 1 to 4, 512 in all within a row
- projector: bfloat16 [16384, 2048], P('row'), may hold values from -0.046875 to 0.046875
- student: bfloat16 [8, 384, 2048], P('col'), may hold values from -6 to 6
Outputs:
- projected: bfloat16 [8, 384, 2048], P('col', 'row')
- gradient: float32 [16384, 2048], P('row', 'col')
The draws below stay inside these ranges and needn't reach their ends.
Inputs may be any that keep to these rules, and one draw needn't show every extreme that they name: Each row of span_lengths sums to 512, and every row has an entry equal to 4.
All inputs are finite; a program needn't handle non-finite values.
Results may differ from the reference program's by a relative error of at most 0.0052.
Values may be sent and summed in bfloat16 or wider, within the bound.
No kernel may reach another device: no remote copies, remote signals or barrier semaphores. Data moves between devices by JAX's collectives and lax.ppermute only.
A program may use at most 128 MiB of HBM per device.

```python
import math
import jax
import jax.numpy as jnp
import numpy as np
from jax import lax

D = 16384
F = 2048
TLEN = 512
SLEN = 384
SEQS = 8
TOKENS = 4096


def draw_residual(key, part):
    key = jax.random.fold_in(key, 11)
    key_base, key_cols, key_rows = jax.random.split(key, 3)
    columns = jnp.arange(D, dtype=jnp.float32) / D
    col_scale = 10.0 ** (0.5 * columns + 0.5 * jax.random.uniform(key_cols, (D,), jnp.float32))
    row_scale = 10.0 ** jax.random.uniform(key_rows, (TOKENS, 1), jnp.float32)
    base = jax.random.normal(key_base, (TOKENS, D), jnp.float32)
    return (base * row_scale * col_scale[None, :] * 0.1).astype(jnp.bfloat16)


def level_of(key, shape, pieces, low, high):
    gain = 1.0
    for position, blocks in pieces:
        heights = jax.random.uniform(jax.random.fold_in(jax.random.fold_in(key, 6), position), (blocks,), jnp.float32, low / len(pieces), high / len(pieces))
        gain = gain * jnp.repeat(jnp.exp(heights), shape[position] // blocks).reshape((-1,) + (1,) * (len(shape) - 1 - position))
    return gain


def length_profile(amount, total, reach, slope):
    weights = [(1 << 20) // math.isqrt(rank ** slope) + 1 for rank in range(2, amount + 1)]
    rest, given = total - reach - (amount - 1), [1] * (amount - 1)
    while rest > 0:
        free = [i for i in range(amount - 1) if given[i] < reach]
        pool, budget = sum([weights[i] for i in free]), rest
        for i in free:
            extra = min(reach - given[i], max(1, budget * weights[i] // pool), rest)
            given[i] = given[i] + extra
            rest = rest - extra
    return np.array([reach] + given)


def uneven(stream_key, amount, total, bound, slope):
    if amount == 2:
        one = jax.random.randint(stream_key, (), max(1, total - bound), min(bound, total - 1) + 1)
        return jnp.stack([one, total - one])
    tallies = jnp.asarray(length_profile(amount, total, bound, slope), jnp.int32)
    couples = (amount - 1) // 2
    giver, sink = tallies[1:1 + 2 * couples:2], tallies[2:2 + 2 * couples:2]
    margin = jnp.minimum(giver - 1, bound - sink)
    passed = jax.random.randint(jax.random.fold_in(stream_key, 1), (couples,), 0, 1 << 20) % (margin + 1)
    tallies = tallies.at[1:1 + 2 * couples:2].set(giver - passed).at[2:2 + 2 * couples:2].set(sink + passed)
    return tallies[jax.random.permutation(jax.random.fold_in(stream_key, 2), amount)]


def scatter_about(own_key, extent, scale, most, cuts=(), kind=jnp.bfloat16):
    drawn = jax.random.normal(own_key, extent, jnp.float32) * scale
    if len(cuts) > 0:
        drawn = level_of(own_key, extent, cuts, -0.22, 0.18) * drawn
    return jnp.clip(drawn, min=-most, max=most).astype(kind)


def setup_inputs(seed: int = 0) -> dict:
    arg_keys = jax.random.split(jax.random.key(seed), 8)
    return {
        "context": scatter_about(arg_keys[0], (TOKENS, D), 1.0, 6.0, ((0, 16), (1, 8))),
        "out_weight": scatter_about(arg_keys[1], (D, D), D ** -0.5, 0.046875, ((0, 8), (1, 16))),
        "residual": draw_residual(jax.random.fold_in(arg_keys[7], 71), 0),
        "norm_gain": jnp.clip(1.0 + 0.15 * jax.random.normal(arg_keys[3], (D,), jnp.float32), 0.25, 1.75),
        "span_lengths": jax.vmap(lambda own: uneven(own, SLEN, TLEN, 4, 1))(jax.random.split(arg_keys[4], SEQS)).reshape((SEQS, SLEN)).astype(jnp.int32),
        "projector": scatter_about(arg_keys[5], (D, F), D ** -0.5, 0.046875, ((0, 16),)),
        "student": scatter_about(arg_keys[6], (SEQS, SLEN, F), 1.0, 6.0, ((0, 8),)),
    }


def reference(context, out_weight, residual, norm_gain, span_lengths, projector, student):
    attended = jnp.dot(context, out_weight, preferred_element_type=jnp.float32)
    stream = residual.astype(jnp.float32) + attended
    mean_square = lax.optimization_barrier(jnp.mean(stream * stream, axis=1))
    hidden = (stream * lax.rsqrt(mean_square + 1e-05)[:, None] * norm_gain.astype(jnp.float32)[None, :]).astype(jnp.bfloat16)
    hidden_seq = hidden.reshape(SEQS, TLEN, D)
    span_ends = jnp.cumsum(span_lengths, axis=1).astype(jnp.int32)
    span_starts = (span_ends - span_lengths).astype(jnp.int32)
    positions = jnp.arange(TLEN, dtype=jnp.int32)
    member = ((positions[None, None, :] >= span_starts[:, :, None]) & (positions[None, None, :] < span_ends[:, :, None])).astype(jnp.float32)
    summed = jnp.einsum('qst,qtd->qsd', member, hidden_seq.astype(jnp.float32))
    pooled = (summed / span_lengths.astype(jnp.float32)[:, :, None]).astype(jnp.bfloat16)
    full_proj = jnp.einsum('qsd,df->qsf', pooled.astype(jnp.float32), projector.astype(jnp.float32))
    mismatch = (full_proj - student.astype(jnp.float32)).astype(jnp.bfloat16)
    gradient = jnp.einsum('qsd,qsf->df', pooled.astype(jnp.float32), mismatch.astype(jnp.float32))
    gradient = gradient * (1.0 / math.sqrt(SEQS * SLEN))
    return (full_proj.astype(jnp.bfloat16), gradient)
```

```python
import math

import jax
import jax.numpy as jnp
from jax import lax
from jax.sharding import PartitionSpec as P

F32 = jnp.float32
BF16 = jnp.bfloat16
GROUPS = 4


def body(context, out_weight, residual, norm_gain, span_lengths, projector, student):
    rows, cols = lax.axis_size("row"), lax.axis_size("col")
    xs, ys = rows // 4, cols // 2
    row, col = lax.axis_index("row"), lax.axis_index("col")
    x, zh, core = row // 4, (row // 2) % 2, row % 2
    y, zl = col // 2, col % 2

    def by_row(move):
        return [(i, move(i)) for i in range(rows)]

    def by_col(move):
        return [(i, move(i)) for i in range(cols)]

    x_up, x_down = by_row(lambda i: (i + 4) % rows), by_row(lambda i: (i - 4) % rows)
    x_far = by_row(lambda i: (i + 8) % rows)
    z_far, twin = by_row(lambda i: i ^ 2), by_row(lambda i: i ^ 1)
    y_up, y_down = by_col(lambda i: (i + 2) % cols), by_col(lambda i: (i - 2) % cols)
    y_far, z_near = by_col(lambda i: (i + 4) % cols), by_col(lambda i: i ^ 1)

    def over_row(value, pairs):
        return lax.ppermute(value, "row", pairs)

    def over_col(value, pairs):
        return lax.ppermute(value, "col", pairs)

    def ring_gather(own, send, up, down):
        half = own.shape[0] // 2
        from_below, from_above = send(own, up), send(own, down)
        far = jnp.concatenate([send(from_below[:half], up), send(from_above[half:], down)])
        return [own, from_above, far, from_below]

    def ring_scatter(left, right, send, up, down):
        low, high = send(left[2].astype(BF16), up), send(right[2].astype(BF16), down)
        to_up = jnp.stack([(left[1].astype(F32) + low.astype(F32)).astype(BF16), right[1].astype(BF16)])
        to_down = jnp.stack([left[3].astype(BF16), (right[3].astype(F32) + high.astype(F32)).astype(BF16)])
        below, above = send(to_up, up).astype(F32), send(to_down, down).astype(F32)
        return left[0].astype(F32) + below[0] + above[0], right[0].astype(F32) + below[1] + above[1]

    shard, depth = context.shape
    run = shard // GROUPS
    pieces = context.reshape(GROUPS // 2, 2, run, depth)
    kept = lax.dynamic_index_in_dim(pieces, core, 1, keepdims=False)
    given = lax.dynamic_index_in_dim(pieces, 1 - core, 1, keepdims=False)
    got = over_row(given, twin)
    dealt = jnp.where(core == 0, jnp.concatenate([kept, got]), jnp.concatenate([got, kept]))
    weight_twin = over_row(out_weight, twin)
    first_far = over_row(dealt[:1], z_far)
    rest_far = over_row(dealt[1:], z_far)
    width = out_weight.shape[1]
    keep_near = jnp.bitwise_xor(zl, zh)

    streams = []
    for g in range(GROUPS):
        far = first_far[0] if g == 0 else rest_far[g - 1]
        pair = jnp.concatenate([dealt[g], far])
        tokens = jnp.concatenate(ring_gather(pair, over_row, x_up, x_down))
        mine = jnp.dot(tokens, out_weight, preferred_element_type=F32).astype(BF16)
        other = jnp.dot(tokens, weight_twin, preferred_element_type=F32).astype(BF16)
        mine, other = mine.reshape(xs, 2 * run, width), other.reshape(xs, 2 * run, width)

        def toward(terms, k):
            return lax.dynamic_index_in_dim(terms, (y + k - x + xs) % xs, 0, keepdims=False)

        total = ring_scatter(
            [toward(mine, k) for k in range(ys)],
            [toward(other, k) for k in range(ys)],
            over_col,
            y_up,
            y_down,
        )
        total = jnp.stack(total).reshape(2, 2, run, width)
        held = lax.dynamic_index_in_dim(total, keep_near, 1, keepdims=False)
        away = lax.dynamic_index_in_dim(total, 1 - keep_near, 1, keepdims=False)
        attended = held + over_col(away.astype(BF16), z_near).astype(F32)
        swapped = over_row(attended[1], twin)
        ordered = jnp.where(
            core == 0,
            jnp.concatenate([attended[0], swapped]),
            jnp.concatenate([swapped, attended[0]]),
        )
        streams.append(residual[2 * run * g : 2 * run * (g + 1)].astype(F32) + ordered)
    stream = jnp.concatenate(streams)
    squares = jnp.sum(stream * stream, axis=1)
    squares = squares + over_row(squares, twin)
    squares = squares + over_row(squares, x_up) + over_row(squares, x_down) + over_row(squares, x_far)
    squares = squares + over_row(squares, z_far)
    inverse_rms = lax.rsqrt(squares / (width * rows) + 1e-05)
    hidden = (stream * inverse_rms[:, None] * norm_gain[None, :]).astype(BF16)

    span_sizes = span_lengths[0]
    span_ends = jnp.cumsum(span_sizes)
    count = span_sizes.shape[0]
    block = count // rows
    spans = jnp.stack([span_ends - span_sizes, span_ends, span_sizes]).reshape(3, xs, 2, 2, block)
    spans = jnp.where(core == 0, spans, spans[:, :, :, ::-1])
    spans = jnp.where(zh == 0, spans, spans[:, :, ::-1])
    spans = lax.dynamic_slice_in_dim(jnp.concatenate([spans, spans], axis=1), x, xs, 1)
    starts, ends, sizes = spans.reshape(3, count)
    positions = jnp.arange(stream.shape[0], dtype=jnp.int32)
    member = (positions[None, :] >= starts[:, None]) & (positions[None, :] < ends[:, None])
    summed = jnp.dot(member.astype(BF16), hidden, preferred_element_type=F32)
    pooled = (summed / sizes.astype(F32)[:, None]).astype(BF16)

    all_pooled = jnp.stack(ring_gather(pooled, over_col, y_up, y_down))

    features = projector.shape[1]
    proj = jnp.dot(pooled, projector, preferred_element_type=F32)
    proj = proj.reshape(xs, 2, 2, block, features)
    proj = proj[:, :, 0] + over_row(proj[:, :, 1], twin)
    half = features // 2
    left, right = ring_scatter(
        [proj[k, :, :, :half] for k in range(xs)],
        [proj[k, :, :, half:] for k in range(xs)],
        over_row,
        x_up,
        x_down,
    )
    proj = jnp.concatenate([left, right], axis=2)
    full_proj = proj[0] + over_row(proj[1], z_far)
    student_rows = lax.dynamic_slice_in_dim(student[0], row * block, block, 0)
    mismatch = (full_proj - student_rows.astype(F32)).astype(BF16)

    by_owner = mismatch.reshape(block, ys, 2, features // cols)
    by_owner = jnp.where(zl == 0, by_owner, by_owner[:, :, ::-1]).reshape(block, ys, features // ys)

    def quarter(k):
        return lax.dynamic_index_in_dim(by_owner, (y + k) % ys, 1, keepdims=False)

    part = jnp.stack(
        [
            quarter(0),
            over_col(quarter(3), y_down),
            over_col(quarter(2), y_far),
            over_col(quarter(1), y_up),
        ]
    )
    part = jnp.stack([part, over_row(part, z_far)])
    part = jnp.stack(ring_gather(part, over_row, x_up, x_down))
    part = jnp.stack([part, over_row(part, twin)])
    part = part.transpose(3, 1, 2, 0, 4, 5).reshape(ys * count, features // ys)
    all_pooled = all_pooled.reshape(ys * count, width)
    loss_factor = 1.0 / math.sqrt(cols * count)

    def outer(columns):
        product = lax.dot_general(
            all_pooled, columns, (((0,), (0,)), ((), ())), preferred_element_type=F32
        )
        return product * loss_factor

    own = features // cols
    theirs = over_col(outer(part[:, own:]).astype(BF16), z_near)
    gradient = outer(part[:, :own]) + theirs.astype(F32)
    return (full_proj.astype(BF16)[None], gradient)


def solution(mesh):
    placed = (
        P("row", "col"),
        P("col", "row"),
        P("col", "row"),
        P("row"),
        P("col", None),
        P("row", None),
        P("col", None, None),
    )
    return jax.shard_map(
        body,
        mesh=mesh,
        in_specs=placed,
        out_specs=(P("col", "row", None), P("row", "col")),
        check_vma=False,
    )
```

```python
import math

import jax
import jax.numpy as jnp
from jax import lax
from jax.sharding import PartitionSpec as P

F32 = jnp.float32
BF16 = jnp.bfloat16
RUNS = (64, 64)


def body(context, out_weight, residual, norm_gain, span_lengths, projector, student):
    rows, cols = lax.axis_size("row"), lax.axis_size("col")
    xs, ys = rows // 4, cols // 2
    row, col = lax.axis_index("row"), lax.axis_index("col")
    x, zh, core = row // 4, (row // 2) % 2, row % 2
    y, zl = col // 2, col % 2

    near, following = 1 + 2 * core, 3 - 2 * core
    masks = (0, near, following, 2)

    def mask(r, second):
        return 1 if (r % 2 == 0) != second else 3

    def by_row(move):
        return [(r, move(r)) for r in range(rows)]

    def by_both(move):
        return [(r * cols + c, r * cols + move(r, c)) for r in range(rows) for c in range(cols)]

    x_near = by_row(lambda r: (r // 4 ^ mask(r, False)) * 4 + r % 4)
    x_next = by_row(lambda r: (r // 4 ^ mask(r, True)) * 4 + r % 4)
    y_near = by_both(lambda r, c: (c // 2 ^ mask(r, False)) * 2 + c % 2)
    y_next = by_both(lambda r, c: (c // 2 ^ mask(r, True)) * 2 + c % 2)
    z_far, twin = by_row(lambda r: r ^ 2), by_row(lambda r: r ^ 1)
    y_far = [(c, c ^ 4) for c in range(cols)]
    z_near = [(c, c ^ 1) for c in range(cols)]

    def over_row(value, pairs):
        return lax.ppermute(value, "row", pairs)

    def over_col(value, pairs):
        return lax.ppermute(value, "col", pairs)

    def over_both(value, pairs):
        return lax.ppermute(value, ("row", "col"), pairs)

    def tie(*values):
        return lax.optimization_barrier(values)

    def middle_exchanged(value, axis):
        return jnp.take(value, jnp.array([0, 2, 1, 3]), axis=axis)

    def place_of(distance):
        return jnp.where(distance == 0, 0, jnp.where(distance == 2, 3, jnp.where(distance == near, 1, 2)))

    shard, depth = context.shape
    width = out_weight.shape[1]
    head = shard - sum(RUNS)
    weight_twin = over_row(out_weight, twin)
    first, later = context[:head], context[head:]
    paired = over_row(first, x_near)
    first_far = over_row(first, z_far)
    later_far = over_row(later, z_far)
    paired, weight_twin = tie(paired, weight_twin)
    weight = jnp.concatenate([out_weight, weight_twin], axis=1)

    def later_unit(j):
        span = slice(sum(RUNS[:j]), sum(RUNS[: j + 1]))
        return jnp.concatenate([later[span], later_far[span]])

    def toward(terms, distance):
        place = place_of(jnp.bitwise_xor(jnp.bitwise_xor(y, distance), x))
        return lax.dynamic_index_in_dim(terms, place, 0, keepdims=False)

    def second_of(terms, arrived):
        kept = [
            toward(terms, k).astype(F32) + arrived[i].astype(F32) for i, k in enumerate((0, near))
        ]
        return kept[0], over_both(kept[1].astype(BF16), y_near)

    units, unit, coming = 2 + len(RUNS), first, first_far
    halves, firsts, seconds, all_terms = ([None] * units for _ in range(4))
    for j in range(units):
        if j >= 2:
            paired, all_terms[j - 2] = tie(paired, all_terms[j - 2])
        lane = jnp.concatenate([unit, paired])
        others = over_row(lane, x_next)
        if j == 0:
            others, later_far = tie(others, later_far)
        if j + 1 < units:
            coming, lane = tie(coming, lane)
            coming_paired = over_row(coming, x_near)
        tokens = jnp.concatenate([lane, others])
        terms = jnp.dot(tokens, weight, preferred_element_type=F32).astype(BF16)
        if 1 <= j < units - 1:
            terms, firsts[j - 1] = tie(terms, firsts[j - 1])
        if 2 <= j < units - 1:
            terms, seconds[j - 2] = tie(terms, seconds[j - 2])
        all_terms[j] = terms.reshape(xs, -1, 2 * width)
        firsts[j] = over_both(
            jnp.stack([toward(all_terms[j], following), toward(all_terms[j], 2)]), y_next
        )
        if j >= 1:
            halves[j - 1], seconds[j - 1] = second_of(all_terms[j - 1], firsts[j - 1])
        if j + 1 < units:
            unit, paired = coming, coming_paired
        if j + 2 < units:
            coming = later_unit(j)
    halves[-1], seconds[-1] = second_of(all_terms[-1], firsts[-1])
    sums = [half + second.astype(F32) for half, second in zip(halves, seconds)]

    same = zl == zh
    attended = []
    pairs = [(sums[0], sums[1])] + [(value[:run], value[run:]) for value, run in zip(sums[2:], RUNS)]
    for own, other in pairs:
        held, away = jnp.where(same, own, other), jnp.where(same, other, own)
        attended.append(held + over_col(away.astype(BF16), z_near).astype(F32))
    held = jnp.concatenate([value[:, :width] for value in attended])
    swapped = jnp.concatenate([over_row(value[:, width:], twin) for value in attended])
    attended = jnp.where(core == 0, jnp.concatenate([held, swapped]), jnp.concatenate([swapped, held]))
    stream = attended + residual.astype(F32)

    squares = jnp.sum(stream * stream, axis=1)
    for pairs in (twin, x_near, x_next, z_far):
        squares = squares + over_row(squares, pairs)
    inverse_rms = lax.rsqrt(squares / (width * rows) + 1e-05)
    hidden = (stream * inverse_rms[:, None] * norm_gain[None, :]).astype(BF16)

    span_sizes = span_lengths[0]
    span_ends = jnp.cumsum(span_sizes)
    count = span_sizes.shape[0]
    block = count // rows
    spans = jnp.stack([span_ends - span_sizes, span_ends, span_sizes]).reshape(3, xs, 2, 2, block)
    spans = jnp.where(core == 0, spans, spans[:, :, :, ::-1])
    spans = jnp.where(zh == 0, spans, spans[:, :, ::-1])
    spans = [lax.dynamic_slice_in_dim(spans, jnp.bitwise_xor(x, k), 1, 1) for k in masks]
    starts, ends, sizes = jnp.concatenate(spans, axis=1).reshape(3, count)
    positions = jnp.arange(stream.shape[0], dtype=jnp.int32)
    member = (positions[None, :] >= starts[:, None]) & (positions[None, :] < ends[:, None])
    summed = jnp.dot(member.astype(BF16), hidden, preferred_element_type=F32)
    pooled = (summed / sizes.astype(F32)[:, None]).astype(BF16)
    pooled_near = over_both(pooled, y_near)

    features = projector.shape[1]
    proj = jnp.dot(pooled, projector, preferred_element_type=F32).reshape(xs, 2, 2, block, features)
    proj = proj[:, :, 0] + over_row(middle_exchanged(proj[:, :, 1].astype(BF16), 0), twin).astype(F32)
    arrived = over_row(proj[2:].astype(BF16), x_next)
    proj = proj[:2] + arrived.astype(F32)
    arrived, pooled_near = tie(over_row(proj[1].astype(BF16), x_near), pooled_near)
    pooled_lane = jnp.concatenate([pooled, pooled_near])
    pooled_rest = over_both(pooled_lane, y_next)
    proj = proj[0] + arrived.astype(F32)
    full_proj = proj + over_row(proj[::-1].astype(BF16), z_far).astype(F32)
    places = [x * 4 + jnp.bitwise_xor(zh, kz) * 2 + core for kz in range(2)]
    student_rows = [lax.dynamic_slice_in_dim(student[0], place * block, block, 0) for place in places]
    mismatch = (full_proj - jnp.stack(student_rows).astype(F32)).astype(BF16)

    by_owner = mismatch.reshape(2 * block, ys, 2, features // cols)
    by_owner = jnp.where(zl == 0, by_owner, by_owner[:, :, ::-1]).reshape(2 * block, ys, features // ys)

    def quarter(distance):
        return lax.dynamic_index_in_dim(by_owner, jnp.bitwise_xor(y, distance), 1, keepdims=False)

    part = [
        quarter(0),
        over_both(quarter(near), y_near),
        over_both(quarter(following), y_next),
        over_col(quarter(2), y_far),
    ]
    part = jnp.stack(part)[None]
    part = jnp.concatenate([part, over_row(part, x_near)])
    others, pooled_rest = tie(over_row(part, x_next), pooled_rest)
    part = jnp.concatenate([part, others])
    twin_part = middle_exchanged(middle_exchanged(over_row(part, twin), 0), 1)
    part = jnp.stack([part, twin_part]).reshape(2, xs, ys, 2, block, features // ys)
    part = part.transpose(2, 1, 3, 0, 4, 5).reshape(ys * count, features // ys)
    all_pooled = jnp.concatenate([pooled_lane, pooled_rest])
    loss_factor = 1.0 / math.sqrt(cols * count)

    def outer(columns):
        product = lax.dot_general(
            all_pooled, columns, (((0,), (0,)), ((), ())), preferred_element_type=F32
        )
        return product * loss_factor

    own = features // cols
    theirs = over_col(outer(part[:, own:]).astype(BF16), z_near)
    ours, theirs = tie(outer(part[:, :own]), theirs)
    gradient = ours + theirs.astype(F32)
    return (full_proj[0].astype(BF16)[None], gradient)


def solution(mesh):
    placed = (
        P("row", "col"),
        P("col", "row"),
        P("col", "row"),
        P("row"),
        P("col", None),
        P("row", None),
        P("col", None, None),
    )
    return jax.shard_map(
        body,
        mesh=mesh,
        in_specs=placed,
        out_specs=(P("col", "row", None), P("row", "col")),
        check_vma=False,
    )
```

```python
import math

import jax
import jax.numpy as jnp
from jax import lax
from jax.sharding import PartitionSpec as P

F32 = jnp.float32
BF16 = jnp.bfloat16
RUNS = (64, 64)


def body(context, out_weight, residual, norm_gain, span_lengths, projector, student):
    rows, cols = lax.axis_size("row"), lax.axis_size("col")
    xs, ys = rows // 4, cols // 2
    row, col = lax.axis_index("row"), lax.axis_index("col")
    x, zh, core = row // 4, (row // 2) % 2, row % 2
    y, zl = col // 2, col % 2

    near, following = 1 + 2 * core, 3 - 2 * core
    masks = (0, near, following, 2)

    def mask(r, second):
        return 1 if (r % 2 == 0) != second else 3

    def by_row(move):
        return [(r, move(r)) for r in range(rows)]

    def by_both(move):
        return [(r * cols + c, r * cols + move(r, c)) for r in range(rows) for c in range(cols)]

    x_near = by_row(lambda r: (r // 4 ^ mask(r, False)) * 4 + r % 4)
    x_next = by_row(lambda r: (r // 4 ^ mask(r, True)) * 4 + r % 4)
    y_near = by_both(lambda r, c: (c // 2 ^ mask(r, False)) * 2 + c % 2)
    y_next = by_both(lambda r, c: (c // 2 ^ mask(r, True)) * 2 + c % 2)
    z_far, twin = by_row(lambda r: r ^ 2), by_row(lambda r: r ^ 1)
    y_far = [(c, c ^ 4) for c in range(cols)]
    z_near = [(c, c ^ 1) for c in range(cols)]

    def over_row(value, pairs):
        return lax.ppermute(value, "row", pairs)

    def over_col(value, pairs):
        return lax.ppermute(value, "col", pairs)

    def over_both(value, pairs):
        return lax.ppermute(value, ("row", "col"), pairs)

    def tie(*values):
        return lax.optimization_barrier(values)

    def middle_exchanged(value, axis):
        places = [lax.slice_in_dim(value, k, k + 1, axis=axis) for k in (0, 2, 1, 3)]
        return jnp.concatenate(places, axis=axis)

    def place_of(distance):
        return jnp.where(distance == 0, 0, jnp.where(distance == 2, 3, jnp.where(distance == near, 1, 2)))

    shard, depth = context.shape
    width = out_weight.shape[1]
    head = shard - sum(RUNS)
    weight_twin = over_row(out_weight, twin)
    first, later = context[:head], context[head:]
    paired = over_row(first, x_near)
    first_far = over_row(first, z_far)
    later_far = over_row(later, z_far)
    paired, weight_twin = tie(paired, weight_twin)
    weight = jnp.concatenate([out_weight, weight_twin], axis=1)

    def later_unit(j):
        span = slice(sum(RUNS[:j]), sum(RUNS[: j + 1]))
        return jnp.concatenate([later[span], later_far[span]])

    def toward(terms, distance):
        place = place_of(jnp.bitwise_xor(jnp.bitwise_xor(y, distance), x))
        return lax.dynamic_index_in_dim(terms, place, 0, keepdims=False)

    def second_of(terms, arrived):
        kept = [
            toward(terms, k).astype(F32) + arrived[i].astype(F32) for i, k in enumerate((0, near))
        ]
        return kept[0], over_both(kept[1].astype(BF16), y_near)

    units, unit, coming = 2 + len(RUNS), first, first_far
    halves, firsts, seconds, all_terms = ([None] * units for _ in range(4))
    for j in range(units):
        if j >= 2:
            paired, all_terms[j - 2] = tie(paired, all_terms[j - 2])
        lane = jnp.concatenate([unit, paired])
        others = over_row(lane, x_next)
        if j == 0:
            others, later_far = tie(others, later_far)
        if j + 1 < units:
            coming, lane = tie(coming, lane)
            coming_paired = over_row(coming, x_near)
        tokens = jnp.concatenate([lane, others])
        terms = jnp.dot(tokens, weight, preferred_element_type=F32).astype(BF16)
        if 1 <= j < units - 1:
            terms, firsts[j - 1] = tie(terms, firsts[j - 1])
        if 2 <= j < units - 1:
            terms, seconds[j - 2] = tie(terms, seconds[j - 2])
        all_terms[j] = terms.reshape(xs, -1, 2 * width)
        firsts[j] = over_both(
            jnp.stack([toward(all_terms[j], following), toward(all_terms[j], 2)]), y_next
        )
        if j >= 1:
            halves[j - 1], seconds[j - 1] = second_of(all_terms[j - 1], firsts[j - 1])
        if j + 1 < units:
            unit, paired = coming, coming_paired
        if j + 2 < units:
            coming = later_unit(j)
    halves[-1], seconds[-1] = second_of(all_terms[-1], firsts[-1])
    sums = [half + second.astype(F32) for half, second in zip(halves, seconds)]

    same = zl == zh
    attended = []
    pairs = [(sums[0], sums[1])] + [(value[:run], value[run:]) for value, run in zip(sums[2:], RUNS)]
    for own, other in pairs:
        held, away = jnp.where(same, own, other), jnp.where(same, other, own)
        attended.append(held + over_col(away.astype(BF16), z_near).astype(F32))
    held = jnp.concatenate([value[:, :width] for value in attended])
    swapped = jnp.concatenate([over_row(value[:, width:], twin) for value in attended])
    attended = jnp.where(core == 0, jnp.concatenate([held, swapped]), jnp.concatenate([swapped, held]))
    stream = attended + residual.astype(F32)

    squares = jnp.sum(stream * stream, axis=1)
    for pairs in (twin, x_near, x_next, z_far):
        squares = squares + over_row(squares, pairs)
    inverse_rms = lax.rsqrt(squares / (width * rows) + 1e-05)
    hidden = (stream * inverse_rms[:, None] * norm_gain[None, :]).astype(BF16)

    span_sizes = span_lengths[0]
    span_ends = jnp.cumsum(span_sizes)
    count = span_sizes.shape[0]
    block = count // rows
    spans = jnp.stack([span_ends - span_sizes, span_ends, span_sizes]).reshape(3, xs, 2, 2, block)
    spans = jnp.where(core == 0, spans, spans[:, :, :, ::-1])
    spans = jnp.where(zh == 0, spans, spans[:, :, ::-1])
    spans = [
        lax.dynamic_slice_in_dim(spans[:, :, :, kc], jnp.bitwise_xor(x, k), 1, 1)
        for kc, order in enumerate((masks, (0, following, near, 2)))
        for k in order
    ]
    starts, ends, sizes = jnp.concatenate(spans, axis=1).reshape(3, count)
    positions = jnp.arange(stream.shape[0], dtype=jnp.int32)
    member = (positions[None, :] >= starts[:, None]) & (positions[None, :] < ends[:, None])
    summed = jnp.dot(member.astype(BF16), hidden, preferred_element_type=F32)
    pooled = (summed / sizes.astype(F32)[:, None]).astype(BF16)
    pooled_near = over_both(pooled, y_near)

    features = projector.shape[1]
    given = jnp.dot(pooled[count // 2 :], projector, preferred_element_type=F32).astype(BF16)
    got = over_row(given, twin)
    proj = jnp.dot(pooled[: count // 2], projector, preferred_element_type=F32) + got.astype(F32)
    proj = proj.reshape(xs, 2, block, features)
    arrived = over_row(proj[2:].astype(BF16), x_next)
    proj = proj[:2] + arrived.astype(F32)
    arrived, pooled_near = tie(over_row(proj[1].astype(BF16), x_near), pooled_near)
    proj = proj[0] + arrived.astype(F32)
    full_proj = proj + over_row(proj[::-1].astype(BF16), z_far).astype(F32)
    places = [x * 4 + jnp.bitwise_xor(zh, kz) * 2 + core for kz in range(2)]
    student_rows = [lax.dynamic_slice_in_dim(student[0], place * block, block, 0) for place in places]
    mismatch = (full_proj - jnp.stack(student_rows).astype(F32)).astype(BF16)

    mismatch = mismatch.reshape(2 * block, features)

    def quarter(distance):
        first_column = jnp.bitwise_xor(y, distance) * (features // ys)
        return lax.dynamic_slice_in_dim(mismatch, first_column, features // ys, 1)

    part = [
        quarter(0),
        over_both(quarter(near), y_near),
        over_both(quarter(following), y_next),
        over_col(quarter(2), y_far),
    ]
    part, pooled_near = tie(part, pooled_near)
    pooled_lane = jnp.concatenate([pooled, pooled_near])
    pooled_rest = over_both(pooled_lane, y_next)
    part = jnp.stack(part)[None]
    paired = over_row(part, x_near)
    part = jnp.concatenate([part, paired])
    others = over_row(part, x_next)
    others, pooled_rest = tie(others, pooled_rest)
    part = jnp.concatenate([part, others])
    twin_part = middle_exchanged(over_row(part, twin), 1)
    part = jnp.stack([part, twin_part]).transpose(2, 0, 1, 3, 4)
    part = part.reshape(ys * count, features // ys)
    all_pooled = jnp.concatenate([pooled_lane, pooled_rest])
    loss_factor = 1.0 / math.sqrt(cols * count)

    def outer(columns):
        product = lax.dot_general(
            all_pooled, columns, (((0,), (0,)), ((), ())), preferred_element_type=F32
        )
        return product * loss_factor

    own = features // cols
    theirs = over_col(outer(lax.dynamic_slice_in_dim(part, (1 - zl) * own, own, 1)).astype(BF16), z_near)
    ours, theirs = tie(outer(lax.dynamic_slice_in_dim(part, zl * own, own, 1)), theirs)
    gradient = ours + theirs.astype(F32)
    return (full_proj[0].astype(BF16)[None], gradient)


def solution(mesh):
    placed = (
        P("row", "col"),
        P("col", "row"),
        P("col", "row"),
        P("row"),
        P("col", None),
        P("row", None),
        P("col", None, None),
    )
    return jax.shard_map(
        body,
        mesh=mesh,
        in_specs=placed,
        out_specs=(P("col", "row", None), P("row", "col")),
        check_vma=False,
    )
```

```python
import math

import jax
import jax.numpy as jnp
from jax import lax
from jax.sharding import PartitionSpec as P

F32 = jnp.float32
BF16 = jnp.bfloat16
RUNS = (64, 64)
Z_FIRST = 2


def body(context, out_weight, residual, norm_gain, span_lengths, projector, student):
    rows, cols = lax.axis_size("row"), lax.axis_size("col")
    xs, ys = rows // 4, cols // 2
    row, col = lax.axis_index("row"), lax.axis_index("col")
    x, zh, core = row // 4, (row // 2) % 2, row % 2
    y, zl = col // 2, col % 2

    near, following = 1 + 2 * core, 3 - 2 * core
    masks = (0, near, following, 2)

    def mask(r, second):
        return 1 if (r % 2 == 0) != second else 3

    def by_row(move):
        return [(r, move(r)) for r in range(rows)]

    def by_both(move):
        return [(r * cols + c, r * cols + move(r, c)) for r in range(rows) for c in range(cols)]

    x_near = by_row(lambda r: (r // 4 ^ mask(r, False)) * 4 + r % 4)
    x_next = by_row(lambda r: (r // 4 ^ mask(r, True)) * 4 + r % 4)
    y_near = by_both(lambda r, c: (c // 2 ^ mask(r, False)) * 2 + c % 2)
    y_next = by_both(lambda r, c: (c // 2 ^ mask(r, True)) * 2 + c % 2)
    z_far, twin = by_row(lambda r: r ^ 2), by_row(lambda r: r ^ 1)
    y_far = [(c, c ^ 4) for c in range(cols)]
    z_near = [(c, c ^ 1) for c in range(cols)]

    def over_row(value, pairs):
        return lax.ppermute(value, "row", pairs)

    def over_col(value, pairs):
        return lax.ppermute(value, "col", pairs)

    def over_both(value, pairs):
        return lax.ppermute(value, ("row", "col"), pairs)

    def tie(*values):
        return lax.optimization_barrier(values)

    def middle_exchanged(value, axis):
        places = [lax.slice_in_dim(value, k, k + 1, axis=axis) for k in (0, 2, 1, 3)]
        return jnp.concatenate(places, axis=axis)

    def place_of(distance):
        return jnp.where(distance == 0, 0, jnp.where(distance == 2, 3, jnp.where(distance == near, 1, 2)))

    shard, depth = context.shape
    width = out_weight.shape[1]
    head = shard - sum(RUNS)
    weight_twin = over_row(out_weight, twin)
    first, later = context[:head], context[head:]
    paired = over_row(first, x_near)
    first_far = over_row(first, z_far)
    later_far = over_row(later, z_far)
    paired, weight_twin = tie(paired, weight_twin)
    weight = jnp.concatenate([out_weight, weight_twin], axis=1)

    def later_unit(j):
        span = slice(sum(RUNS[:j]), sum(RUNS[: j + 1]))
        return jnp.concatenate([later[span], later_far[span]])

    def toward(terms, distance):
        place = place_of(jnp.bitwise_xor(jnp.bitwise_xor(y, distance), x))
        return lax.dynamic_index_in_dim(terms, place, 0, keepdims=False)

    def second_of(terms, arrived):
        kept = [
            toward(terms, k).astype(F32) + arrived[i].astype(F32) for i, k in enumerate((0, near))
        ]
        return kept[0], over_both(kept[1].astype(BF16), y_near)

    same = zl == zh
    units, unit, coming = 2 + len(RUNS), first, first_far
    halves, firsts, seconds, all_terms = ([None] * units for _ in range(4))
    for j in range(units):
        if j >= 2:
            paired, all_terms[j - 2] = tie(paired, all_terms[j - 2])
        lane = jnp.concatenate([unit, paired])
        others = over_row(lane, x_next)
        if j == 0:
            others, later_far = tie(others, later_far)
        if j + 1 < units:
            coming, lane = tie(coming, lane)
            coming_paired = over_row(coming, x_near)
        tokens = jnp.concatenate([lane, others])
        terms = jnp.dot(tokens, weight, preferred_element_type=F32).astype(BF16)
        if 1 <= j < units - 1:
            terms, firsts[j - 1] = tie(terms, firsts[j - 1])
        if 2 <= j < units - 1:
            terms, seconds[j - 2] = tie(terms, seconds[j - 2])
        all_terms[j] = terms.reshape(xs, -1, 2 * width)
        if j == Z_FIRST:
            own, other = all_terms[j][:, : RUNS[j - 2]], all_terms[j][:, RUNS[j - 2] :]
            held, away = jnp.where(same, own, other), jnp.where(same, other, own)
            held = held.astype(F32) + over_col(away, z_near).astype(F32)
            all_terms[j] = held.astype(BF16)
        firsts[j] = over_both(
            jnp.stack([toward(all_terms[j], following), toward(all_terms[j], 2)]), y_next
        )
        if j >= 1:
            halves[j - 1], seconds[j - 1] = second_of(all_terms[j - 1], firsts[j - 1])
        if j + 1 < units:
            unit, paired = coming, coming_paired
        if j + 2 < units:
            coming = later_unit(j)
    halves[-1], seconds[-1] = second_of(all_terms[-1], firsts[-1])
    sums = [half + second.astype(F32) for half, second in zip(halves, seconds)]

    attended = []
    pairs = [(sums[0], sums[1])] + [(value[:run], value[run:]) for value, run in zip(sums[2:], RUNS)]
    for j, (own, other) in enumerate(pairs):
        if j + 1 == Z_FIRST:
            attended.append(sums[j + 1])
            continue
        held, away = jnp.where(same, own, other), jnp.where(same, other, own)
        attended.append(held + over_col(away.astype(BF16), z_near).astype(F32))
    held = jnp.concatenate([value[:, :width] for value in attended])
    swapped = jnp.concatenate([over_row(value[:, width:], twin) for value in attended])
    attended = jnp.where(core == 0, jnp.concatenate([held, swapped]), jnp.concatenate([swapped, held]))
    stream = attended + residual.astype(F32)

    squares = jnp.sum(stream * stream, axis=1)
    for pairs in (twin, x_near, x_next, z_far):
        squares = squares + over_row(squares, pairs)
    inverse_rms = lax.rsqrt(squares / (width * rows) + 1e-05)
    hidden = (stream * inverse_rms[:, None] * norm_gain[None, :]).astype(BF16)

    span_sizes = span_lengths[0]
    span_ends = jnp.cumsum(span_sizes)
    count = span_sizes.shape[0]
    block = count // rows
    spans = jnp.stack([span_ends - span_sizes, span_ends, span_sizes]).reshape(3, xs, 2, 2, block)
    spans = jnp.where(core == 0, spans, spans[:, :, :, ::-1])
    spans = jnp.where(zh == 0, spans, spans[:, :, ::-1])
    spans = [
        lax.dynamic_slice_in_dim(spans[:, :, :, kc], jnp.bitwise_xor(x, k), 1, 1)
        for kc, order in enumerate((masks, (0, following, near, 2)))
        for k in order
    ]
    starts, ends, sizes = jnp.concatenate(spans, axis=1).reshape(3, count)
    positions = jnp.arange(stream.shape[0], dtype=jnp.int32)
    member = (positions[None, :] >= starts[:, None]) & (positions[None, :] < ends[:, None])
    summed = jnp.dot(member.astype(BF16), hidden, preferred_element_type=F32)
    pooled = (summed / sizes.astype(F32)[:, None]).astype(BF16)
    pooled_near = over_both(pooled, y_near)

    features = projector.shape[1]
    given = jnp.dot(pooled[count // 2 :], projector, preferred_element_type=F32).astype(BF16)
    got = over_row(given, twin)
    proj = jnp.dot(pooled[: count // 2], projector, preferred_element_type=F32) + got.astype(F32)
    proj = proj.reshape(xs, 2, block, features)
    arrived = over_row(proj[2:].astype(BF16), x_next)
    proj = proj[:2] + arrived.astype(F32)
    arrived, pooled_near = tie(over_row(proj[1].astype(BF16), x_near), pooled_near)
    proj = proj[0] + arrived.astype(F32)
    full_proj = proj + over_row(proj[::-1].astype(BF16), z_far).astype(F32)
    places = [x * 4 + jnp.bitwise_xor(zh, kz) * 2 + core for kz in range(2)]
    student_rows = [lax.dynamic_slice_in_dim(student[0], place * block, block, 0) for place in places]
    mismatch = (full_proj - jnp.stack(student_rows).astype(F32)).astype(BF16)

    mismatch = mismatch.reshape(2 * block, features)

    def quarter(distance):
        first_column = jnp.bitwise_xor(y, distance) * (features // ys)
        return lax.dynamic_slice_in_dim(mismatch, first_column, features // ys, 1)

    part = [
        quarter(0),
        over_both(quarter(near), y_near),
        over_both(quarter(following), y_next),
        over_col(quarter(2), y_far),
    ]
    part, pooled_near = tie(part, pooled_near)
    pooled_lane = jnp.concatenate([pooled, pooled_near])
    pooled_rest = over_both(pooled_lane, y_next)
    part = jnp.stack(part)[None]
    paired = over_row(part, x_near)
    part = jnp.concatenate([part, paired])
    others = over_row(part, x_next)
    others, pooled_rest = tie(others, pooled_rest)
    part = jnp.concatenate([part, others])
    twin_part = middle_exchanged(over_row(part, twin), 1)
    part = jnp.stack([part, twin_part]).transpose(2, 0, 1, 3, 4)
    part = part.reshape(ys * count, features // ys)
    all_pooled = jnp.concatenate([pooled_lane, pooled_rest])
    loss_factor = 1.0 / math.sqrt(cols * count)

    def outer(columns):
        product = lax.dot_general(
            all_pooled, columns, (((0,), (0,)), ((), ())), preferred_element_type=F32
        )
        return product * loss_factor

    own = features // cols
    theirs = over_col(outer(lax.dynamic_slice_in_dim(part, (1 - zl) * own, own, 1)).astype(BF16), z_near)
    ours, theirs = tie(outer(lax.dynamic_slice_in_dim(part, zl * own, own, 1)), theirs)
    gradient = ours + theirs.astype(F32)
    return (full_proj[0].astype(BF16)[None], gradient)


def solution(mesh):
    placed = (
        P("row", "col"),
        P("col", "row"),
        P("col", "row"),
        P("row"),
        P("col", None),
        P("row", None),
        P("col", None, None),
    )
    return jax.shard_map(
        body,
        mesh=mesh,
        in_specs=placed,
        out_specs=(P("col", "row", None), P("row", "col")),
        check_vma=False,
    )
```

```python
import math

import jax
import jax.numpy as jnp
from jax import lax
from jax.sharding import PartitionSpec as P

F32 = jnp.float32
BF16 = jnp.bfloat16
RUNS = (64, 64)


def body(context, out_weight, residual, norm_gain, span_lengths, projector, student):
    rows, cols = lax.axis_size("row"), lax.axis_size("col")
    xs, ys = rows // 4, cols // 2
    row, col = lax.axis_index("row"), lax.axis_index("col")
    x, zh, core = row // 4, (row // 2) % 2, row % 2
    y, zl = col // 2, col % 2

    near, following = 1 + 2 * core, 3 - 2 * core
    masks = (0, near, following, 2)

    def mask(r, second):
        return 1 if (r % 2 == 0) != second else 3

    def by_row(move):
        return [(r, move(r)) for r in range(rows)]

    def by_both(move):
        return [(r * cols + c, r * cols + move(r, c)) for r in range(rows) for c in range(cols)]

    x_near = by_row(lambda r: (r // 4 ^ mask(r, False)) * 4 + r % 4)
    x_next = by_row(lambda r: (r // 4 ^ mask(r, True)) * 4 + r % 4)
    y_near = by_both(lambda r, c: (c // 2 ^ mask(r, False)) * 2 + c % 2)
    y_next = by_both(lambda r, c: (c // 2 ^ mask(r, True)) * 2 + c % 2)
    z_far, twin = by_row(lambda r: r ^ 2), by_row(lambda r: r ^ 1)
    y_far = [(c, c ^ 4) for c in range(cols)]
    z_near = [(c, c ^ 1) for c in range(cols)]

    def over_row(value, pairs):
        return lax.ppermute(value, "row", pairs)

    def over_col(value, pairs):
        return lax.ppermute(value, "col", pairs)

    def over_both(value, pairs):
        return lax.ppermute(value, ("row", "col"), pairs)

    def tie(*values):
        return lax.optimization_barrier(values)

    def middle_exchanged(value, axis):
        places = [lax.slice_in_dim(value, k, k + 1, axis=axis) for k in (0, 2, 1, 3)]
        return jnp.concatenate(places, axis=axis)

    def place_of(distance):
        return jnp.where(distance == 0, 0, jnp.where(distance == 2, 3, jnp.where(distance == near, 1, 2)))

    shard, depth = context.shape
    width = out_weight.shape[1]
    head = shard - sum(RUNS)
    weight_twin = over_row(out_weight, twin)
    first, later = context[:head], context[head:]
    paired = over_row(first, x_near)
    first_far = over_row(first, z_far)
    later_far = over_row(later, z_far)
    paired, weight_twin = tie(paired, weight_twin)
    weight = jnp.concatenate([out_weight, weight_twin], axis=1)

    def later_unit(j):
        span = slice(sum(RUNS[:j]), sum(RUNS[: j + 1]))
        return jnp.concatenate([later[span], later_far[span]])

    def toward(terms, distance):
        place = place_of(jnp.bitwise_xor(jnp.bitwise_xor(y, distance), x))
        return lax.dynamic_index_in_dim(terms, place, 0, keepdims=False)

    def second_of(terms, arrived):
        kept = [
            toward(terms, k).astype(F32) + arrived[i].astype(F32) for i, k in enumerate((0, near))
        ]
        return kept[0], over_both(kept[1].astype(BF16), y_near)

    same = zl == zh
    units, unit, coming = 2 + len(RUNS), first, first_far
    halves, firsts, seconds, all_terms = ([None] * units for _ in range(4))
    for j in range(units):
        if j >= 2 and j - 2 != units - 2:
            paired, all_terms[j - 2] = tie(paired, all_terms[j - 2])
        lane = jnp.concatenate([unit, paired])
        others = over_row(lane, x_next)
        if j == 0:
            others, later_far = tie(others, later_far)
        if j + 1 < units:
            coming, lane = tie(coming, lane)
            coming_paired = over_row(coming, x_near)
        tokens = jnp.concatenate([lane, others])
        terms = jnp.dot(tokens, weight, preferred_element_type=F32).astype(BF16)
        arrived_pair = coming_paired if j + 1 < units else None
        arrived_unit = coming
        if j + 2 < units:
            coming = later_unit(j)
        z_first = j == units - 2
        if z_first:
            by_place = terms.reshape(xs, 2, RUNS[j - 2], 2 * width)
            held, away = (
                lax.dynamic_index_in_dim(by_place, place, 1, keepdims=False)
                for place in (jnp.bitwise_xor(zl, zh), 1 - jnp.bitwise_xor(zl, zh))
            )
            swapped = over_col(away, z_near)
            held, firsts[j - 1], seconds[j - 2] = tie(held, firsts[j - 1], seconds[j - 2])
            terms = held, swapped
        elif j == 1:
            terms, firsts[j - 1] = tie(terms, firsts[j - 1])
        all_terms[j] = terms if z_first else terms.reshape(xs, -1, 2 * width)
        if z_first:
            if j + 1 < units:
                unit, paired = arrived_unit, arrived_pair
            halves[j - 1], seconds[j - 1] = second_of(all_terms[j - 1], firsts[j - 1])
            continue
        firsts[j] = over_both(
            jnp.stack([toward(all_terms[j], following), toward(all_terms[j], 2)]), y_next
        )
        if j >= 1 and j - 1 != units - 2:
            halves[j - 1], seconds[j - 1] = second_of(all_terms[j - 1], firsts[j - 1])
        if j + 1 < units:
            unit, paired = arrived_unit, arrived_pair
    held, swapped = all_terms[-2]
    swapped, firsts[-1] = tie(swapped, firsts[-1])
    halves[-1], seconds[-1] = second_of(all_terms[-1], firsts[-1])
    all_terms[-2] = (held.astype(F32) + swapped.astype(F32)).astype(BF16)
    firsts[-2] = over_both(
        jnp.stack([toward(all_terms[-2], following), toward(all_terms[-2], 2)]), y_next
    )
    halves[-2], seconds[-2] = second_of(all_terms[-2], firsts[-2])
    sums = [half + second.astype(F32) for half, second in zip(halves, seconds)]

    attended = []
    pairs = [(sums[0], sums[1])] + [(value[:run], value[run:]) for value, run in zip(sums[2:], RUNS)]
    for j, (own, other) in enumerate(pairs):
        if j + 1 == units - 2:
            attended.append(sums[j + 1])
            continue
        held, away = jnp.where(same, own, other), jnp.where(same, other, own)
        attended.append(held + over_col(away.astype(BF16), z_near).astype(F32))
    held = jnp.concatenate([value[:, :width] for value in attended])
    swapped = jnp.concatenate([over_row(value[:, width:], twin) for value in attended])
    attended = jnp.where(core == 0, jnp.concatenate([held, swapped]), jnp.concatenate([swapped, held]))
    stream = attended + residual.astype(F32)

    squares = jnp.sum(stream * stream, axis=1)
    for pairs in (twin, x_near, x_next, z_far):
        squares = squares + over_row(squares, pairs)
    inverse_rms = lax.rsqrt(squares / (width * rows) + 1e-05)
    hidden = (stream * inverse_rms[:, None] * norm_gain[None, :]).astype(BF16)

    span_sizes = span_lengths[0]
    span_ends = jnp.cumsum(span_sizes)
    count = span_sizes.shape[0]
    block = count // rows
    spans = jnp.stack([span_ends - span_sizes, span_ends, span_sizes]).reshape(3, xs, 2, 2, block)
    spans = jnp.where(core == 0, spans, spans[:, :, :, ::-1])
    spans = jnp.where(zh == 0, spans, spans[:, :, ::-1])
    spans = [
        lax.dynamic_slice_in_dim(spans[:, :, :, kc], jnp.bitwise_xor(x, k), 1, 1)
        for kc, order in enumerate((masks, (0, following, near, 2)))
        for k in order
    ]
    starts, ends, sizes = jnp.concatenate(spans, axis=1).reshape(3, count)
    positions = jnp.arange(stream.shape[0], dtype=jnp.int32)
    member = (positions[None, :] >= starts[:, None]) & (positions[None, :] < ends[:, None])
    summed = jnp.dot(member.astype(BF16), hidden, preferred_element_type=F32)
    pooled = (summed / sizes.astype(F32)[:, None]).astype(BF16)
    pooled_near, pooled_next = over_both(pooled, y_near), over_both(pooled, y_next)

    features = projector.shape[1]
    given = jnp.dot(pooled[count // 2 :], projector, preferred_element_type=F32).astype(BF16)
    got = over_row(given, twin)
    proj = jnp.dot(pooled[: count // 2], projector, preferred_element_type=F32) + got.astype(F32)
    proj = proj.reshape(xs, 2, block, features)
    arrived = over_row(proj[2:].astype(BF16), x_next)
    proj = proj[:2] + arrived.astype(F32)
    proj = proj[0] + over_row(proj[1].astype(BF16), x_near).astype(F32)
    full_proj = proj + over_row(proj[::-1].astype(BF16), z_far).astype(F32)
    places = [x * 4 + jnp.bitwise_xor(zh, kz) * 2 + core for kz in range(2)]
    student_rows = [lax.dynamic_slice_in_dim(student[0], place * block, block, 0) for place in places]
    mismatch = (full_proj - jnp.stack(student_rows).astype(F32)).astype(BF16)

    mismatch = mismatch.reshape(2 * block, features)

    def quarter(distance):
        first_column = jnp.bitwise_xor(y, distance) * (features // ys)
        return lax.dynamic_slice_in_dim(mismatch, first_column, features // ys, 1)

    part = [
        quarter(0),
        over_both(quarter(near), y_near),
        over_both(quarter(following), y_next),
        over_col(quarter(2), y_far),
    ]
    part, pooled_near, pooled_next = tie(part, pooled_near, pooled_next)
    pooled_lane = jnp.concatenate([pooled, pooled_near, pooled_next])
    pooled_rest = over_both(pooled_near, y_next)
    part = jnp.stack(part)[None]
    paired = over_row(part, x_near)
    part = jnp.concatenate([part, paired])
    others = over_row(part, x_next)
    others, pooled_rest = tie(others, pooled_rest)
    part = jnp.concatenate([part, others])
    twin_part = middle_exchanged(over_row(part, twin), 1)
    part = jnp.stack([part, twin_part]).transpose(2, 0, 1, 3, 4)
    part = part.reshape(ys * count, features // ys)
    all_pooled = jnp.concatenate([pooled_lane, pooled_rest])
    loss_factor = 1.0 / math.sqrt(cols * count)

    def outer(columns):
        product = lax.dot_general(
            all_pooled, columns, (((0,), (0,)), ((), ())), preferred_element_type=F32
        )
        return product * loss_factor

    own = features // cols
    theirs = over_col(outer(lax.dynamic_slice_in_dim(part, (1 - zl) * own, own, 1)).astype(BF16), z_near)
    ours, theirs = tie(outer(lax.dynamic_slice_in_dim(part, zl * own, own, 1)), theirs)
    gradient = ours + theirs.astype(F32)
    return (full_proj[0].astype(BF16)[None], gradient)


def solution(mesh):
    placed = (
        P("row", "col"),
        P("col", "row"),
        P("col", "row"),
        P("row"),
        P("col", None),
        P("row", None),
        P("col", None, None),
    )
    return jax.shard_map(
        body,
        mesh=mesh,
        in_specs=placed,
        out_specs=(P("col", "row", None), P("row", "col")),
        check_vma=False,
    )
```

```python
import math

import jax
import jax.numpy as jnp
from jax import lax
from jax.sharding import PartitionSpec as P

F32 = jnp.float32
BF16 = jnp.bfloat16
RUNS = (64, 64)


def body(context, out_weight, residual, norm_gain, span_lengths, projector, student):
    rows, cols = lax.axis_size("row"), lax.axis_size("col")
    xs, ys = rows // 4, cols // 2
    row, col = lax.axis_index("row"), lax.axis_index("col")
    x, zh, core = row // 4, (row // 2) % 2, row % 2
    y, zl = col // 2, col % 2

    near, following = 1 + 2 * core, 3 - 2 * core
    masks = (0, near, following, 2)

    def mask(r, second):
        return 1 if (r % 2 == 0) != second else 3

    def by_row(move):
        return [(r, move(r)) for r in range(rows)]

    def by_both(move):
        return [(r * cols + c, r * cols + move(r, c)) for r in range(rows) for c in range(cols)]

    x_near = by_row(lambda r: (r // 4 ^ mask(r, False)) * 4 + r % 4)
    x_next = by_row(lambda r: (r // 4 ^ mask(r, True)) * 4 + r % 4)
    y_near = by_both(lambda r, c: (c // 2 ^ mask(r, False)) * 2 + c % 2)
    y_next = by_both(lambda r, c: (c // 2 ^ mask(r, True)) * 2 + c % 2)
    z_far, twin = by_row(lambda r: r ^ 2), by_row(lambda r: r ^ 1)
    y_far = [(c, c ^ 4) for c in range(cols)]
    z_near = [(c, c ^ 1) for c in range(cols)]

    def over_row(value, pairs):
        return lax.ppermute(value, "row", pairs)

    def over_col(value, pairs):
        return lax.ppermute(value, "col", pairs)

    def over_both(value, pairs):
        return lax.ppermute(value, ("row", "col"), pairs)

    def tie(*values):
        return lax.optimization_barrier(values)

    def middle_exchanged(value, axis):
        places = [lax.slice_in_dim(value, k, k + 1, axis=axis) for k in (0, 2, 1, 3)]
        return jnp.concatenate(places, axis=axis)

    def place_of(distance):
        return jnp.where(distance == 0, 0, jnp.where(distance == 2, 3, jnp.where(distance == near, 1, 2)))

    shard, depth = context.shape
    width = out_weight.shape[1]
    head = shard - sum(RUNS)
    weight_twin = over_row(out_weight, twin)
    first, later = context[:head], context[head:]
    paired = over_row(first, x_near)
    first_far = over_row(first, z_far)
    later_far = over_row(later, z_far)
    paired, weight_twin = tie(paired, weight_twin)
    weight = jnp.concatenate([out_weight, weight_twin], axis=1)

    def later_unit(j):
        span = slice(sum(RUNS[:j]), sum(RUNS[: j + 1]))
        return jnp.concatenate([later[span], later_far[span]])

    def toward(terms, distance):
        place = place_of(jnp.bitwise_xor(jnp.bitwise_xor(y, distance), x))
        return lax.dynamic_index_in_dim(terms, place, 0, keepdims=False)

    def second_of(terms, arrived):
        kept = [
            toward(terms, k).astype(F32) + arrived[i].astype(F32) for i, k in enumerate((0, near))
        ]
        return kept[0], over_both(kept[1].astype(BF16), y_near)

    same = zl == zh
    units, unit, coming = 2 + len(RUNS), first, first_far
    halves, firsts, seconds, all_terms = ([None] * units for _ in range(4))
    for j in range(units):
        if j >= 3 and j - 2 != units - 2:
            paired, all_terms[j - 2] = tie(paired, all_terms[j - 2])
        lane = jnp.concatenate([unit, paired])
        others = over_row(lane, x_next)
        if j == 0:
            others, later_far = tie(others, later_far)
        if j + 1 < units:
            coming, lane = tie(coming, lane)
            coming_paired = over_row(coming, x_near)
        tokens = jnp.concatenate([lane, others])
        terms = jnp.dot(tokens, weight, preferred_element_type=F32).astype(BF16)
        arrived_pair = coming_paired if j + 1 < units else None
        arrived_unit = coming
        if j + 2 < units:
            coming = later_unit(j)
        z_first = j == units - 2
        if z_first:
            by_place = terms.reshape(xs, 2, RUNS[j - 2], 2 * width)
            held, away = (
                lax.dynamic_index_in_dim(by_place, place, 1, keepdims=False)
                for place in (jnp.bitwise_xor(zl, zh), 1 - jnp.bitwise_xor(zl, zh))
            )
            swapped = over_col(away, z_near)
            held, firsts[j - 1], seconds[j - 2] = tie(held, firsts[j - 1], seconds[j - 2])
            terms = held, swapped
        elif j == 1:
            terms, firsts[j - 1] = tie(terms, firsts[j - 1])
        all_terms[j] = terms if z_first else terms.reshape(xs, -1, 2 * width)
        if z_first:
            if j + 1 < units:
                unit, paired = arrived_unit, arrived_pair
            halves[j - 1], seconds[j - 1] = second_of(all_terms[j - 1], firsts[j - 1])
            continue
        firsts[j] = over_both(
            jnp.stack([toward(all_terms[j], following), toward(all_terms[j], 2)]), y_next
        )
        if j >= 1 and j - 1 != units - 2:
            halves[j - 1], seconds[j - 1] = second_of(all_terms[j - 1], firsts[j - 1])
        if j + 1 < units:
            unit, paired = arrived_unit, arrived_pair
    held, swapped = all_terms[-2]
    swapped, firsts[-1] = tie(swapped, firsts[-1])
    halves[-1], seconds[-1] = second_of(all_terms[-1], firsts[-1])
    all_terms[-2] = (held.astype(F32) + swapped.astype(F32)).astype(BF16)
    firsts[-2] = over_both(
        jnp.stack([toward(all_terms[-2], following), toward(all_terms[-2], 2)]), y_next
    )
    halves[-2], seconds[-2] = second_of(all_terms[-2], firsts[-2])
    sums = [half + second.astype(F32) for half, second in zip(halves, seconds)]

    attended = []
    pairs = [(sums[0], sums[1])] + [(value[:run], value[run:]) for value, run in zip(sums[2:], RUNS)]
    for j, (own, other) in enumerate(pairs):
        if j + 1 == units - 2:
            attended.append(sums[j + 1])
            continue
        held, away = jnp.where(same, own, other), jnp.where(same, other, own)
        attended.append(held + over_col(away.astype(BF16), z_near).astype(F32))
    held = jnp.concatenate([value[:, :width] for value in attended])
    swapped = jnp.concatenate([over_row(value[:, width:], twin) for value in attended])
    attended = jnp.where(core == 0, jnp.concatenate([held, swapped]), jnp.concatenate([swapped, held]))
    stream = attended + residual.astype(F32)

    squares = jnp.sum(stream * stream, axis=1)
    for pairs in (twin, x_near, x_next, z_far):
        squares = squares + over_row(squares, pairs)
    inverse_rms = lax.rsqrt(squares / (width * rows) + 1e-05)
    hidden = (stream * inverse_rms[:, None] * norm_gain[None, :]).astype(BF16)

    span_sizes = span_lengths[0]
    span_ends = jnp.cumsum(span_sizes)
    count = span_sizes.shape[0]
    block = count // rows
    spans = jnp.stack([span_ends - span_sizes, span_ends, span_sizes]).reshape(3, xs, 2, 2, block)
    spans = jnp.where(core == 0, spans, spans[:, :, :, ::-1])
    spans = jnp.where(zh == 0, spans, spans[:, :, ::-1])
    spans = [
        lax.dynamic_slice_in_dim(spans[:, :, :, kc], jnp.bitwise_xor(x, k), 1, 1)
        for kc, order in enumerate((masks, (0, following, near, 2)))
        for k in order
    ]
    starts, ends, sizes = jnp.concatenate(spans, axis=1).reshape(3, count)
    positions = jnp.arange(stream.shape[0], dtype=jnp.int32)
    member = (positions[None, :] >= starts[:, None]) & (positions[None, :] < ends[:, None])
    summed = jnp.dot(member.astype(BF16), hidden, preferred_element_type=F32)
    pooled = (summed / sizes.astype(F32)[:, None]).astype(BF16)
    pooled_near, pooled_next = over_both(pooled, y_near), over_both(pooled, y_next)

    features = projector.shape[1]
    given = jnp.dot(pooled[count // 2 :], projector, preferred_element_type=F32).astype(BF16)
    got = over_row(given, twin)
    proj = jnp.dot(pooled[: count // 2], projector, preferred_element_type=F32) + got.astype(F32)
    proj = proj.reshape(xs, 2, block, features)
    arrived = over_row(proj[2:].astype(BF16), x_next)
    proj = proj[:2] + arrived.astype(F32)
    proj = proj[0] + over_row(proj[1].astype(BF16), x_near).astype(F32)
    full_proj = proj + over_row(proj[::-1].astype(BF16), z_far).astype(F32)
    places = [x * 4 + jnp.bitwise_xor(zh, kz) * 2 + core for kz in range(2)]
    student_rows = [lax.dynamic_slice_in_dim(student[0], place * block, block, 0) for place in places]
    mismatch = (full_proj - jnp.stack(student_rows).astype(F32)).astype(BF16)

    mismatch = mismatch.reshape(2 * block, features)

    def quarter(distance):
        first_column = jnp.bitwise_xor(y, distance) * (features // ys)
        return lax.dynamic_slice_in_dim(mismatch, first_column, features // ys, 1)

    part = [
        quarter(0),
        over_both(quarter(near), y_near),
        over_both(quarter(following), y_next),
        over_col(quarter(2), y_far),
    ]
    part, pooled_near, pooled_next = tie(part, pooled_near, pooled_next)
    pooled_lane = jnp.concatenate([pooled, pooled_near, pooled_next])
    pooled_rest = over_both(pooled_near, y_next)
    part = jnp.stack(part)[None]
    paired = over_row(part, x_near)
    part = jnp.concatenate([part, paired])
    others = over_row(part, x_next)
    others, pooled_rest = tie(others, pooled_rest)
    part = jnp.concatenate([part, others])
    twin_part = middle_exchanged(over_row(part, twin), 1)
    part = jnp.stack([part, twin_part])
    all_pooled = jnp.concatenate([pooled_lane, pooled_rest])
    loss_factor = 1.0 / math.sqrt(cols * count)

    def outer(columns):
        product = lax.dot_general(
            all_pooled, columns, (((0,), (0,)), ((), ())), preferred_element_type=F32
        )
        return product * loss_factor

    own = features // cols
    def columns_of(place):
        columns = lax.dynamic_slice_in_dim(part, place * own, own, part.ndim - 1)
        return columns.transpose(2, 0, 1, 3, 4).reshape(ys * count, own)

    theirs, ours = columns_of(1 - zl), columns_of(zl)
    (theirs,) = tie(theirs)
    theirs = over_col(outer(theirs).astype(BF16), z_near)
    ours, theirs = tie(outer(ours), theirs)
    gradient = ours + theirs.astype(F32)
    return (full_proj[0].astype(BF16)[None], gradient)


def solution(mesh):
    placed = (
        P("row", "col"),
        P("col", "row"),
        P("col", "row"),
        P("row"),
        P("col", None),
        P("row", None),
        P("col", None, None),
    )
    return jax.shard_map(
        body,
        mesh=mesh,
        in_specs=placed,
        out_specs=(P("col", "row", None), P("row", "col")),
        check_vma=False,
    )
```

```python
import math

import jax
import jax.numpy as jnp
from jax import lax
from jax.sharding import PartitionSpec as P

F32 = jnp.float32
BF16 = jnp.bfloat16
RUNS = (64, 64)


def body(context, out_weight, residual, norm_gain, span_lengths, projector, student):
    rows, cols = lax.axis_size("row"), lax.axis_size("col")
    xs, ys = rows // 4, cols // 2
    row, col = lax.axis_index("row"), lax.axis_index("col")
    x, zh, core = row // 4, (row // 2) % 2, row % 2
    y, zl = col // 2, col % 2

    near, following = 1 + 2 * core, 3 - 2 * core
    masks = (0, near, following, 2)

    def mask(r, second):
        return 1 if (r % 2 == 0) != second else 3

    def by_row(move):
        return [(r, move(r)) for r in range(rows)]

    def by_both(move):
        return [(r * cols + c, r * cols + move(r, c)) for r in range(rows) for c in range(cols)]

    x_near = by_row(lambda r: (r // 4 ^ mask(r, False)) * 4 + r % 4)
    x_next = by_row(lambda r: (r // 4 ^ mask(r, True)) * 4 + r % 4)
    y_near = by_both(lambda r, c: (c // 2 ^ mask(r, False)) * 2 + c % 2)
    y_next = by_both(lambda r, c: (c // 2 ^ mask(r, True)) * 2 + c % 2)
    z_far, twin = by_row(lambda r: r ^ 2), by_row(lambda r: r ^ 1)
    y_far = [(c, c ^ 4) for c in range(cols)]
    z_near = [(c, c ^ 1) for c in range(cols)]

    def over_row(value, pairs):
        return lax.ppermute(value, "row", pairs)

    def over_col(value, pairs):
        return lax.ppermute(value, "col", pairs)

    def over_both(value, pairs):
        return lax.ppermute(value, ("row", "col"), pairs)

    def tie(*values):
        return lax.optimization_barrier(values)

    def middle_exchanged(value, axis):
        places = [lax.slice_in_dim(value, k, k + 1, axis=axis) for k in (0, 2, 1, 3)]
        return jnp.concatenate(places, axis=axis)

    def place_of(distance):
        return jnp.where(distance == 0, 0, jnp.where(distance == 2, 3, jnp.where(distance == near, 1, 2)))

    shard, depth = context.shape
    width = out_weight.shape[1]
    head = shard - sum(RUNS)
    weight_twin = over_row(out_weight, twin)
    first, later = context[:head], context[head:]
    paired = over_row(first, x_near)
    first_far = over_row(first, z_far)
    later_far = over_row(later, z_far)
    paired, weight_twin = tie(paired, weight_twin)
    weight = jnp.concatenate([out_weight, weight_twin], axis=1)

    def later_unit(j):
        span = slice(sum(RUNS[:j]), sum(RUNS[: j + 1]))
        return jnp.concatenate([later[span], later_far[span]])

    def toward(terms, distance):
        place = place_of(jnp.bitwise_xor(jnp.bitwise_xor(y, distance), x))
        return lax.dynamic_index_in_dim(terms, place, 0, keepdims=False)

    def second_of(terms, arrived):
        kept = [
            toward(terms, k).astype(F32) + arrived[i].astype(F32) for i, k in enumerate((0, near))
        ]
        return kept[0], over_both(kept[1].astype(BF16), y_near)

    same = zl == zh
    units, unit, coming = 2 + len(RUNS), first, first_far
    halves, firsts, seconds, all_terms = ([None] * units for _ in range(4))
    for j in range(units):
        if j >= 3 and j - 2 != units - 2:
            paired, all_terms[j - 2] = tie(paired, all_terms[j - 2])
        lane = jnp.concatenate([unit, paired])
        others = over_row(lane, x_next)
        if j == 0:
            others, later_far = tie(others, later_far)
        if j + 1 < units:
            coming, lane = tie(coming, lane)
            coming_paired = over_row(coming, x_near)
        tokens = jnp.concatenate([lane, others])
        terms = jnp.dot(tokens, weight, preferred_element_type=F32).astype(BF16)
        arrived_pair = coming_paired if j + 1 < units else None
        arrived_unit = coming
        if j + 2 < units:
            coming = later_unit(j)
        z_first = j == units - 2
        if z_first:
            by_place = terms.reshape(xs, 2, RUNS[j - 2], 2 * width)
            held, away = (
                lax.dynamic_index_in_dim(by_place, place, 1, keepdims=False)
                for place in (jnp.bitwise_xor(zl, zh), 1 - jnp.bitwise_xor(zl, zh))
            )
            swapped = over_col(away, z_near)
            held, firsts[j - 1], seconds[j - 2] = tie(held, firsts[j - 1], seconds[j - 2])
            terms = held, swapped
        elif j == 1:
            terms, firsts[j - 1] = tie(terms, firsts[j - 1])
        all_terms[j] = terms if z_first else terms.reshape(xs, -1, 2 * width)
        if z_first:
            if j + 1 < units:
                unit, paired = arrived_unit, arrived_pair
            halves[j - 1], seconds[j - 1] = second_of(all_terms[j - 1], firsts[j - 1])
            continue
        firsts[j] = over_both(
            jnp.stack([toward(all_terms[j], following), toward(all_terms[j], 2)]), y_next
        )
        if j >= 1 and j - 1 != units - 2:
            halves[j - 1], seconds[j - 1] = second_of(all_terms[j - 1], firsts[j - 1])
        if j + 1 < units:
            unit, paired = arrived_unit, arrived_pair
    held, swapped = all_terms[-2]
    swapped, firsts[-1] = tie(swapped, firsts[-1])
    halves[-1], seconds[-1] = second_of(all_terms[-1], firsts[-1])
    all_terms[-2] = (held.astype(F32) + swapped.astype(F32)).astype(BF16)
    firsts[-2] = over_both(
        jnp.stack([toward(all_terms[-2], following), toward(all_terms[-2], 2)]), y_next
    )
    halves[-2], seconds[-2] = second_of(all_terms[-2], firsts[-2])
    sums = [half + second.astype(F32) for half, second in zip(halves, seconds)]

    attended = []
    pairs = [(sums[0], sums[1])] + [(value[:run], value[run:]) for value, run in zip(sums[2:], RUNS)]
    for j, (own, other) in enumerate(pairs):
        if j + 1 == units - 2:
            attended.append(sums[j + 1])
            continue
        held, away = jnp.where(same, own, other), jnp.where(same, other, own)
        attended.append(held + over_col(away.astype(BF16), z_near).astype(F32))
    held = jnp.concatenate([value[:, :width] for value in attended])
    swapped = jnp.concatenate([over_row(value[:, width:], twin) for value in attended])
    attended = jnp.where(core == 0, jnp.concatenate([held, swapped]), jnp.concatenate([swapped, held]))
    stream = attended + residual.astype(F32)

    squares = jnp.sum(stream * stream, axis=1)
    for pairs in (z_far, x_near, x_next, twin):
        squares = squares + over_row(squares, pairs)
    inverse_rms = lax.rsqrt(squares / (width * rows) + 1e-05)
    hidden = (stream * inverse_rms[:, None] * norm_gain[None, :]).astype(BF16)

    span_sizes = span_lengths[0]
    span_ends = jnp.cumsum(span_sizes)
    count = span_sizes.shape[0]
    block = count // rows
    spans = jnp.stack([span_ends - span_sizes, span_ends, span_sizes]).reshape(3, xs, 2, 2, block)
    spans = jnp.where(core == 0, spans, spans[:, :, :, ::-1])
    spans = jnp.where(zh == 0, spans, spans[:, :, ::-1])
    spans = [
        lax.dynamic_slice_in_dim(spans[:, :, :, kc], jnp.bitwise_xor(x, k), 1, 1)
        for kc, order in enumerate((masks, (0, following, near, 2)))
        for k in order
    ]
    starts, ends, sizes = jnp.concatenate(spans, axis=1).reshape(3, count)
    positions = jnp.arange(stream.shape[0], dtype=jnp.int32)
    member = (positions[None, :] >= starts[:, None]) & (positions[None, :] < ends[:, None])
    summed = jnp.dot(member.astype(BF16), hidden, preferred_element_type=F32)
    pooled = (summed / sizes.astype(F32)[:, None]).astype(BF16)
    pooled_near, pooled_next = over_both(pooled, y_near), over_both(pooled, y_next)

    features = projector.shape[1]
    given = jnp.dot(pooled[count // 2 :], projector, preferred_element_type=F32).astype(BF16)
    got = over_row(given, twin)
    proj = jnp.dot(pooled[: count // 2], projector, preferred_element_type=F32) + got.astype(F32)
    proj = proj.reshape(xs, 2, block, features)
    arrived = over_row(proj[2:].astype(BF16), x_next)
    proj = proj[:2] + arrived.astype(F32)
    proj = proj[0] + over_row(proj[1].astype(BF16), x_near).astype(F32)
    full_proj = proj + over_row(proj[::-1].astype(BF16), z_far).astype(F32)
    places = [x * 4 + jnp.bitwise_xor(zh, kz) * 2 + core for kz in range(2)]
    student_rows = [lax.dynamic_slice_in_dim(student[0], place * block, block, 0) for place in places]
    mismatch = (full_proj - jnp.stack(student_rows).astype(F32)).astype(BF16)

    mismatch = mismatch.reshape(2 * block, features)

    def quarter(distance):
        first_column = jnp.bitwise_xor(y, distance) * (features // ys)
        return lax.dynamic_slice_in_dim(mismatch, first_column, features // ys, 1)

    part = [
        quarter(0),
        over_both(quarter(near), y_near),
        over_both(quarter(following), y_next),
        over_col(quarter(2), y_far),
    ]
    part, pooled_near, pooled_next = tie(part, pooled_near, pooled_next)
    pooled_lane = jnp.concatenate([pooled, pooled_near, pooled_next])
    pooled_rest = over_both(pooled_near, y_next)
    part = jnp.stack(part)[None]
    paired = over_row(part, x_near)
    part = jnp.concatenate([part, paired])
    others = over_row(part, x_next)
    others, pooled_rest = tie(others, pooled_rest)
    part = jnp.concatenate([part, others])
    twin_part = middle_exchanged(over_row(part, twin), 1)
    part = jnp.stack([part, twin_part])
    all_pooled = jnp.concatenate([pooled_lane, pooled_rest])
    loss_factor = 1.0 / math.sqrt(cols * count)

    def outer(columns):
        product = lax.dot_general(
            all_pooled, columns, (((0,), (0,)), ((), ())), preferred_element_type=F32
        )
        return product * loss_factor

    own = features // cols
    def columns_of(place):
        columns = lax.dynamic_slice_in_dim(part, place * own, own, part.ndim - 1)
        return columns.transpose(2, 0, 1, 3, 4).reshape(ys * count, own)

    theirs, ours = columns_of(1 - zl), columns_of(zl)
    (theirs,) = tie(theirs)
    theirs = over_col(outer(theirs).astype(BF16), z_near)
    ours, theirs = tie(outer(ours), theirs)
    gradient = ours + theirs.astype(F32)
    return (full_proj[0].astype(BF16)[None], gradient)


def solution(mesh):
    placed = (
        P("row", "col"),
        P("col", "row"),
        P("col", "row"),
        P("row"),
        P("col", None),
        P("row", None),
        P("col", None, None),
    )
    return jax.shard_map(
        body,
        mesh=mesh,
        in_specs=placed,
        out_specs=(P("col", "row", None), P("row", "col")),
        check_vma=False,
    )
```
